128 devices in a mesh: ctx: 32 (over z, x, core), head: 4 (over y).
Axes of the slice: x: 4, y: 4, z: 4, core: 2. Of those that a mesh axis runs over, the one named last changes fastest.
Arguments:
- queries: bfloat16 [131072, 2048], P('ctx', 'head'), may hold values from -6 to 6
- keys: bfloat16 [131072, 2048], P('ctx', 'head'), may hold values from -6 to 6
- values: bfloat16 [131072, 2048], P('ctx', 'head'), may hold values from -6 to 6
- lam_index: int32 [2048], P('ctx'), may hold values from 0 to 15
- level_weights: float32 [16, 16, 12], P(None, 'head'), may hold values from 0.25 to 2
- gate: bfloat16 [131072, 2048], P(('ctx', 'head')), may hold values from -6 to 6
- norm_gain: float32 [2048], replicated, may hold values from 0.25 to 1.75
- out_weight: bfloat16 [2048, 2048], P(None, ('ctx', 'head')), may hold values from -0.125 to 0.125
Outputs:
- output: bfloat16 [131072, 2048], P(('ctx', 'head'))
The draws below stay inside these ranges and needn't reach their ends.
All inputs are finite; a program needn't handle non-finite values.
Results may differ from the reference program's by a relative error of at most 0.0064.
Values may be sent and summed in bfloat16 or wider, within the bound.
A program may use at most 192 MiB of HBM per device.

```python
import math
import jax
import jax.numpy as jnp
from jax import lax

HEADS = 16
DK = 128
D = 2048
SPAN = 64
LEVELS = 12
TABLE = 16
TOKENS = 131072
SPANS = 2048


def touch_ends(drawn, stream_key, least, top_value):
    dims = drawn.shape
    index_at = [jax.random.randint(jax.random.fold_in(stream_key, axis), (), 0, dims[axis]) for axis in range(len(dims))]
    drawn = drawn.at[tuple(index_at)].set(least)
    longest = dims.index(max(dims))
    index_at[longest] = (index_at[longest] + 1) % dims[longest]
    return drawn.at[tuple(index_at)].set(top_value)


def steps_of(key, shape, shards, smallest, high):
    level, own = 1.0, jax.random.fold_in(key, 6)
    for dim, parts in shards:
        heights = jnp.exp(jax.random.uniform(jax.random.fold_in(own, dim), (parts,), jnp.float32, smallest / len(shards), high / len(shards)))
        level = level * jnp.repeat(heights, shape[dim] // parts).reshape([-1 if axis == dim else 1 for axis in range(len(shape))])
    return level


def noise(rng, dims, scale, reach, split=(), kind=jnp.bfloat16):
    result = jax.random.normal(rng, dims, jnp.float32) * scale
    if len(split) > 0:
        result = steps_of(rng, dims, split, -0.22, 0.18) * result
    return jnp.clip(result, min=-reach, max=reach).astype(kind)


def setup_inputs(seed: int = 0) -> dict:
    key_of = jax.random.split(jax.random.key(seed), 9)
    queries = noise(key_of[0], (TOKENS, D), 1.0, 6.0, ((0, 32), (1, 4)))
    keys = noise(key_of[1], (TOKENS, D), 1.0, 6.0, ((0, 32), (1, 4)))
    values = noise(key_of[2], (TOKENS, D), 1.0, 6.0, ((0, 32), (1, 4)))
    lam_index = touch_ends(jax.random.randint(key_of[3], (SPANS,), 0, TABLE), jax.random.fold_in(key_of[3], 1), 0, TABLE - 1).astype(jnp.int32)
    level_weights = jnp.clip(jnp.exp(math.log(2.0) - 2.0794415 * jax.random.uniform(key_of[4], (TABLE, HEADS, LEVELS), jnp.float32) ** steps_of(key_of[4], (TABLE, HEADS, LEVELS), ((1, 4),), -0.2, 0.2)), 0.25, 2.0)
    gate = noise(key_of[5], (TOKENS, D), 1.0, 6.0, ((0, 128),))
    norm_gain = jnp.clip(1.0 + 0.15 * jax.random.normal(key_of[6], (D,), jnp.float32), 0.25, 1.75)
    out_weight = noise(key_of[7], (D, D), D ** -0.5, 0.125, ((1, 128),))
    return dict(queries=queries, keys=keys, values=values, lam_index=lam_index, level_weights=level_weights, gate=gate, norm_gain=norm_gain, out_weight=out_weight)


def tree_mix(span_states, coefficient):
    total_count = span_states.shape[0]
    tail_shape = span_states.shape[1:]
    mixed = jnp.zeros_like(span_states)
    partial_value = span_states
    tree_level = 1
    block_width = 1
    while block_width < total_count:
        pair_count = total_count // (2 * block_width)
        paired = partial_value.reshape((pair_count, 2) + tail_shape)
        weight = coefficient[..., tree_level].reshape((pair_count, 2, block_width) + tail_shape[:-2])[:, 1]
        addend = weight[..., None, None] * paired[:, 0][:, None]
        mixed = mixed.reshape((pair_count, 2, block_width) + tail_shape).at[:, 1].add(addend)
        mixed = mixed.reshape((total_count,) + tail_shape)
        partial_value = paired[:, 0] + paired[:, 1]
        tree_level += 1
        block_width *= 2
    return (mixed, partial_value[0])

def reference(queries, keys, values, lam_index, level_weights, gate, norm_gain, out_weight):
    span_total = TOKENS // SPAN
    level_scale = jnp.exp2(-0.5 * jnp.arange(LEVELS, dtype=jnp.float32)) * DK ** (-0.5)
    coefficient = level_weights[lam_index] * level_scale
    causal = jnp.arange(SPAN)[:, None] >= jnp.arange(SPAN)[None, :]

    def per_head(head_id):
        query_blocks = lax.dynamic_slice_in_dim(queries, head_id * DK, DK, 1).reshape(span_total, SPAN, DK).astype(jnp.float32)
        key_blocks = lax.dynamic_slice_in_dim(keys, head_id * DK, DK, 1).reshape(span_total, SPAN, DK).astype(jnp.float32)
        value_blocks = lax.dynamic_slice_in_dim(values, head_id * DK, DK, 1).reshape(span_total, SPAN, DK).astype(jnp.float32)
        head_coef = coefficient[:, head_id, :]
        span_states = jnp.einsum('ctk,ctv->ckv', key_blocks, value_blocks)
        tree_state, unused_total = tree_mix(span_states, head_coef)
        rounded = lax.optimization_barrier(tree_state.astype(jnp.bfloat16)).astype(jnp.float32)
        carried = jnp.einsum('ctk,ckv->ctv', query_blocks, rounded)
        scores = jnp.einsum('csk,ctk->cst', query_blocks, key_blocks) * head_coef[:, 0][:, None, None]
        local_weights = jnp.where(causal[None], scores, 0.0).astype(jnp.bfloat16)
        local_weights = lax.optimization_barrier(local_weights).astype(jnp.float32)
        local_part = jnp.einsum('cst,ctv->csv', local_weights, value_blocks)
        return (local_part + carried).astype(jnp.bfloat16).reshape(TOKENS, DK)
    head_outputs = lax.map(per_head, jnp.arange(HEADS, dtype=jnp.int32))
    attention = head_outputs.transpose(1, 0, 2).reshape(TOKENS, D)
    gated = attention.astype(jnp.float32) * jax.nn.silu(gate.astype(jnp.float32))
    mean_square = lax.optimization_barrier(jnp.mean(gated * gated, axis=-1, keepdims=True))
    normed = (gated * lax.rsqrt(mean_square + 1e-06) * norm_gain).astype(jnp.bfloat16)
    return jnp.dot(normed, out_weight, preferred_element_type=jnp.float32).astype(jnp.bfloat16)
```

```python
import functools

import jax
import jax.numpy as jnp
from jax import lax
from jax.experimental import pallas as pl
from jax.experimental.pallas import tpu as pltpu
from jax.sharding import PartitionSpec as P

DK = 128
SPAN = 64
LEVELS = 12
GROUP = 4
GR = GROUP * SPAN
SCALE = [2.0 ** (-0.5 * l) * DK**-0.5 for l in range(LEVELS)]
MESH = pl.DeviceIdType.MESH
F32 = jnp.float32
BF16 = jnp.bfloat16
NT = (((1,), (1,)), ((), ()))
TN = (((0,), (0,)), ((), ()))


def partner(i, m):
    if m == 1:
        return i + 1 - 2 * lax.rem(i, 2)
    if m == 2:
        return i + 2 - 4 * (i // 2)
    return 3 - i


def flip(i):
    return i + 1 - 2 * lax.rem(i, 2)


def kernel(
    lam, lw, q_hbm, k_hbm, v_hbm, gate_hbm, gain, w_hbm, out_hbm,
    qv, kv, vv, gv, att, wv, ov, nrm, gst, p2, p4, p8, tot, tsib, cown, csend, crecv, rsend, rrecv, xfull,
    local_sem, ssem, rsem,
):
    ctx = lax.axis_index("ctx")
    y = lax.axis_index("head")
    core = lax.rem(ctx, 2)
    x = lax.rem(ctx // 2, 4)
    z = ctx // 8

    def dev(zz, xx, cc, yy):
        return (zz * 8 + xx * 2 + cc, yy)

    sib = dev(z, x, 1 - core, y)
    xp = {m: dev(z, partner(x, m), core, y) for m in (1, 2, 3)}
    zp = {m: dev(partner(z, m), x, core, y) for m in (1, 2, 3)}
    yp = {m: dev(z, x, core, partner(y, m)) for m in (1, 2, 3)}

    counter = [0]

    def remote(src, dst, device):
        i = counter[0]
        counter[0] += 1
        return pltpu.make_async_remote_copy(
            src_ref=src, dst_ref=dst, send_sem=ssem.at[i], recv_sem=rsem.at[i],
            device_id=device, device_id_type=MESH,
        )

    lcount = [0]

    def local(src, dst):
        i = lcount[0]
        lcount[0] += 1
        return pltpu.make_async_copy(src, dst, local_sem.at[i])

    everything = []

    def go(copies):
        for c in copies:
            c.start()
        everything.extend(copies)
        return copies

    def arrived(copies):
        for c in copies:
            c.wait_recv()

    w_load = local(w_hbm, wv.at[z, x, core, pl.ds(pl.multiple_of(y * 16, 16), 16)])
    w_load.start()
    kv_loads = []
    for c in range(4):
        rows = pl.ds(c * 1024, 1024)
        pair = (local(k_hbm.at[rows], kv.at[rows]), local(v_hbm.at[rows], vv.at[rows]))
        for cp in pair:
            cp.start()
        kv_loads.append(pair)
    q_load = local(q_hbm, qv)
    q_load.start()
    g_load = local(gate_hbm, gv)
    g_load.start()

    barrier = pltpu.get_barrier_semaphore()
    friends = [sib] + [d[m] for d in (xp, zp, yp) for m in (1, 2, 3)]
    for f in friends:
        pl.semaphore_signal(barrier, inc=1, device_id=f, device_id_type=MESH)
    pl.semaphore_wait(barrier, len(friends))

    w_load.wait()
    mine = wv.at[z, x, core, pl.ds(pl.multiple_of(y * 16, 16), 16)]
    wy = go([remote(mine, mine, yp[m]) for m in (1, 2, 3)])

    w1 = None
    for c in range(4):
        for cp in kv_loads[c]:
            cp.wait()

        def states(i, carry):
            g = c * 4 + i
            rows = pl.ds(pl.multiple_of(g * GR, GR), GR)
            for h in range(4):
                cols = slice(h * DK, (h + 1) * DK)
                gst[h, g] = lax.dot_general(kv[rows, cols], vv[rows, cols], TN, preferred_element_type=F32)
            return carry

        lax.fori_loop(0, 4, states, 0)
        for h in range(4):
            p2[h, 2 * c] = gst[h, 4 * c] + gst[h, 4 * c + 1]
            p2[h, 2 * c + 1] = gst[h, 4 * c + 2] + gst[h, 4 * c + 3]
            p4[h, c] = p2[h, 2 * c] + p2[h, 2 * c + 1]
        if c == 1:
            arrived(wy)
            a_own = wv.at[z, x, core, pl.ds(0, 32)]
            b_own = wv.at[z, x, core, pl.ds(32, 32)]
            w1 = go([remote(a_own, a_own, xp[m]) for m in (1, 2, 3)] + [remote(b_own, b_own, zp[m]) for m in (1, 2, 3)])
    for h in range(4):
        p8[h, 0] = p4[h, 0] + p4[h, 1]
        p8[h, 1] = p4[h, 2] + p4[h, 3]
        tot[h] = p8[h, 0] + p8[h, 1]

    half = pl.ds(core * 2, 2)
    t_copy = go([remote(tot, tsib, sib)])
    arrived(t_copy)
    cown[...] = tot[half] + tsib[half]
    csend[...] = cown[...].astype(BF16)
    c_copy = go([remote(csend, crecv.at[m - 1], xp[m]) for m in (1, 2, 3)])
    arrived(c_copy)
    rsend[...] = (
        (cown[...] + crecv[0].astype(F32)) + (crecv[1].astype(F32) + crecv[2].astype(F32))
    ).astype(BF16)
    r_copy = go([remote(rsend, rrecv.at[m - 1], zp[m]) for m in (1, 2, 3)])
    xfull[0, half] = crecv[0].astype(F32)
    xfull[1, half] = crecv[1].astype(F32) + crecv[2].astype(F32)
    x12 = xfull.at[pl.ds(0, 2), half]
    x12_copy = go([remote(x12, x12, sib)])
    arrived(w1)
    w2b_src = wv.at[:, x, core, pl.ds(32, 32)]
    w2b = go([remote(w2b_src, w2b_src, xp[m]) for m in (1, 2, 3)])
    arrived(r_copy)
    xfull[2, half] = rrecv[0].astype(F32)
    xfull[3, half] = rrecv[1].astype(F32) + rrecv[2].astype(F32)
    x34 = xfull.at[pl.ds(2, 2), half]
    x34_copy = go([remote(x34, x34, sib)])
    w2a_src = wv.at[z, :, core, pl.ds(0, 32)]
    w2a = go([remote(w2a_src, w2a_src, zp[m]) for m in (1, 2, 3)])
    arrived(x12_copy)
    arrived(x34_copy)
    fwd = go([remote(s, s, sib) for s in (w2a_src, w2b_src)])
    q_load.wait()

    bits = [core, lax.rem(x, 2), x // 2, lax.rem(z, 2), z // 2]
    cross_bit = [b.astype(F32) for b in bits]
    lane = lax.broadcasted_iota(jnp.int32, (SPAN, DK), 1)
    row = lax.broadcasted_iota(jnp.int32, (SPAN, DK), 0)
    low = lane <= row
    high = lane <= row + SPAN
    left = lane < SPAN

    def attend(g, put):
        rows = pl.ds(pl.multiple_of(g * GR, GR), GR)
        g2, g4, g8 = g // 2, g // 4, g // 8
        own_bit = [lax.rem(b, 2).astype(F32) for b in (g, g2, g4, g8)]
        s1, s2, s4, s8 = flip(g), flip(g2), flip(g4), flip(g8)
        for h in range(4):
            cols = slice(h * DK, (h + 1) * DK)
            qg, kg, vg = qv[rows, cols], kv[rows, cols], vv[rows, cols]
            s = lax.dot_general(qg, kg, NT, preferred_element_type=F32)
            near, far = [], []
            for p in range(GROUP):
                tab = lam[g * GROUP + p]
                w = [lw[l, h, tab] * SCALE[l] for l in range(3)]
                far.append(
                    [lw[3 + i, h, tab] * (SCALE[3 + i] * own_bit[i]) for i in range(4)]
                    + [lw[7 + i, h, tab] * (SCALE[7 + i] * cross_bit[i]) for i in range(5)]
                )
                sp = s[p * SPAN : (p + 1) * SPAN]
                diag = sp[:, (p // 2) * DK : (p // 2 + 1) * DK]
                if p % 2 == 0:
                    diag = jnp.where(low, diag * w[0], 0.0)
                else:
                    diag = jnp.where(high, diag * jnp.where(left, w[1], w[0]), 0.0)
                near.append(
                    diag.astype(BF16)
                    if p < 2
                    else jnp.concatenate([(sp[:, :DK] * w[2]).astype(BF16), diag.astype(BF16)], axis=1)
                )
            part = [
                jnp.dot(jnp.concatenate(near[:2], axis=0), vg[: 2 * SPAN], preferred_element_type=F32),
                jnp.dot(jnp.concatenate(near[2:], axis=0), vg, preferred_element_type=F32),
            ]
            mixed = [[] for _ in range(GROUP)]
            for r in range(0, DK, 32):
                tile = slice(r, r + 32)
                terms = [
                    gst[h, s1, tile, :], p2[h, s2, tile, :], p4[h, s4, tile, :], p8[h, s8, tile, :], tsib[h, tile, :],
                    xfull[0, h, tile, :], xfull[1, h, tile, :], xfull[2, h, tile, :], xfull[3, h, tile, :],
                ]
                for p in range(GROUP):
                    acc = terms[0] * far[p][0]
                    for term, weight in zip(terms[1:], far[p][1:]):
                        acc = acc + term * weight
                    mixed[p].append(acc.astype(BF16))
            res = []
            for p in range(GROUP):
                carried = jnp.dot(
                    qg[p * SPAN : (p + 1) * SPAN], jnp.concatenate(mixed[p], axis=0), preferred_element_type=F32
                )
                res.append((part[p // 2][(p % 2) * SPAN : (p % 2 + 1) * SPAN] + carried).astype(BF16))
            put(cols, rows, jnp.concatenate(res, axis=0))

    att_copies = []
    for j in range(4):
        def to_send(cols, rows, value):
            qv[rows, cols] = value

        def keep(cols, rows, value, j=j):
            att[y, pl.ds(j * GR, GR), cols] = value

        batch = []
        for m in (2, 1, 3):
            g = partner(y, m) * 4 + j
            attend(g, to_send)
            batch += go([
                remote(qv.at[pl.ds(pl.multiple_of(g * GR, GR), GR)], att.at[y, pl.ds(j * GR, GR)], yp[m])
            ])
        att_copies.append(batch)
        attend(y * 4 + j, keep)

    arrived(w2a)
    arrived(w2b)
    for m in (1, 2, 3):
        a = wv.at[partner(z, m), :, core, pl.ds(0, 32)]
        b = wv.at[:, partner(x, m), core, pl.ds(32, 32)]
        fwd += go([remote(a, a, sib), remote(b, b, sib)])
    arrived(fwd)
    g_load.wait()

    stores = []
    for j in range(4):
        arrived(att_copies[j])

        def normalize(i, carry, j=j):
            rows = pl.ds(pl.multiple_of(j * GR + i * 16, 16), 16)
            a = jnp.concatenate([att[s, rows, :] for s in range(4)], axis=1).astype(F32)
            gt = gv[rows, :].astype(F32)
            gated = a * (gt / (1.0 + jnp.exp(-gt)))
            mean = jnp.mean(gated * gated, axis=1, keepdims=True)
            nrm[pl.ds(pl.multiple_of(i * 16, 16), 16), :] = (
                gated * lax.rsqrt(mean + 1e-6) * gain[...]
            ).astype(BF16)
            return carry

        lax.fori_loop(0, GR // 16, normalize, 0)
        for n in range(4):
            w = wv[n].reshape(512, 2048)
            ov[pl.ds(j * GR, GR), n * 512 : (n + 1) * 512] = lax.dot_general(
                nrm[...], w, NT, preferred_element_type=F32
            ).astype(BF16)
        st = local(ov.at[pl.ds(j * GR, GR)], out_hbm.at[pl.ds(j * GR, GR)])
        st.start()
        stores.append(st)

    for st in stores:
        st.wait()
    for c in everything:
        c.wait_send()


def local_step(queries, keys, values, lam_index, level_weights, gate, norm_gain, out_weight):
    any_spec = pl.BlockSpec(memory_space=pl.ANY)
    smem = pl.BlockSpec(memory_space=pltpu.SMEM)
    vmem = pl.BlockSpec(memory_space=pltpu.VMEM)
    return pl.pallas_call(
        kernel,
        out_shape=jax.ShapeDtypeStruct((1024, 2048), BF16),
        in_specs=[smem, smem, any_spec, any_spec, any_spec, any_spec, vmem, any_spec],
        out_specs=any_spec,
        scratch_shapes=[
            pltpu.VMEM((4096, 512), BF16),
            pltpu.VMEM((4096, 512), BF16),
            pltpu.VMEM((4096, 512), BF16),
            pltpu.VMEM((1024, 2048), BF16),
            pltpu.VMEM((4, 1024, 512), BF16),
            pltpu.VMEM((4, 4, 2, 64, 2048), BF16),
            pltpu.VMEM((1024, 2048), BF16),
            pltpu.VMEM((GR, 2048), BF16),
            pltpu.VMEM((4, 16, DK, DK), F32),
            pltpu.VMEM((4, 8, DK, DK), F32),
            pltpu.VMEM((4, 4, DK, DK), F32),
            pltpu.VMEM((4, 2, DK, DK), F32),
            pltpu.VMEM((4, DK, DK), F32),
            pltpu.VMEM((4, DK, DK), F32),
            pltpu.VMEM((2, DK, DK), F32),
            pltpu.VMEM((2, DK, DK), BF16),
            pltpu.VMEM((3, 2, DK, DK), BF16),
            pltpu.VMEM((2, DK, DK), BF16),
            pltpu.VMEM((3, 2, DK, DK), BF16),
            pltpu.VMEM((4, 4, DK, DK), F32),
            pltpu.SemaphoreType.DMA((16,)),
            pltpu.SemaphoreType.DMA((48,)),
            pltpu.SemaphoreType.DMA((48,)),
        ],
        compiler_params=pltpu.CompilerParams(
            collective_id=0, has_side_effects=True, vmem_limit_bytes=58 * 1024 * 1024
        ),
    )(
        lam_index, jnp.transpose(level_weights, (2, 1, 0)), queries, keys, values, gate,
        norm_gain.reshape(1, 2048), jnp.transpose(out_weight),
    )


def solution(mesh):
    in_specs = (
        P("ctx", "head"),
        P("ctx", "head"),
        P("ctx", "head"),
        P("ctx"),
        P(None, "head", None),
        P(("ctx", "head"), None),
        P(),
        P(None, ("ctx", "head")),
    )
    out_specs = P(("ctx", "head"), None)
    return jax.shard_map(local_step, mesh=mesh, in_specs=in_specs, out_specs=out_specs, check_vma=False)
```

```python
import functools

import jax
import jax.numpy as jnp
from jax import lax
from jax.experimental import pallas as pl
from jax.experimental.pallas import tpu as pltpu
from jax.sharding import PartitionSpec as P

DK = 128
SPAN = 64
LEVELS = 12
GROUP = 4
GR = GROUP * SPAN
SCALE = [2.0 ** (-0.5 * l) * DK**-0.5 for l in range(LEVELS)]
MESH = pl.DeviceIdType.MESH
F32 = jnp.float32
UNROLL = True
BF16 = jnp.bfloat16
NT = (((1,), (1,)), ((), ()))
TN = (((0,), (0,)), ((), ()))


def partner(i, m):
    if m == 1:
        return i + 1 - 2 * lax.rem(i, 2)
    if m == 2:
        return i + 2 - 4 * (i // 2)
    return 3 - i


def flip(i):
    return i + 1 - 2 * lax.rem(i, 2)


def kernel(
    lam, lw, q_hbm, k_hbm, v_hbm, gate_hbm, gain, w_hbm, ov, nrm, wv,
    qv, kv, vv, gv, att, gst, p2, p4, p8, tot, tsib, cown, csend, crecv, rsend, rrecv, xfull,
    local_sem, ssem, rsem, att_send, att_recv,
):
    ctx = lax.axis_index("ctx")
    y = lax.axis_index("head")
    core = lax.rem(ctx, 2)
    x = lax.rem(ctx // 2, 4)
    z = ctx // 8

    def dev(zz, xx, cc, yy):
        return (zz * 8 + xx * 2 + cc, yy)

    sib = dev(z, x, 1 - core, y)
    xp = {m: dev(z, partner(x, m), core, y) for m in (1, 2, 3)}
    zp = {m: dev(partner(z, m), x, core, y) for m in (1, 2, 3)}
    yp = {m: dev(z, x, core, partner(y, m)) for m in (1, 2, 3)}

    counter = [0]

    def remote(src, dst, device):
        i = counter[0]
        counter[0] += 1
        return pltpu.make_async_remote_copy(
            src_ref=src, dst_ref=dst, send_sem=ssem.at[i], recv_sem=rsem.at[i],
            device_id=device, device_id_type=MESH,
        )

    lcount = [0]

    def local(src, dst):
        i = lcount[0]
        lcount[0] += 1
        return pltpu.make_async_copy(src, dst, local_sem.at[i])

    everything = []

    def go(copies):
        for c in copies:
            c.start()
        everything.extend(copies)
        return copies

    def arrived(copies):
        for c in copies:
            c.wait_recv()

    w_load = local(w_hbm, wv.at[z, x, core, pl.ds(pl.multiple_of(y * 16, 16), 16)])
    w_load.start()
    kv_loads = []
    for c in range(4):
        rows = pl.ds(c * 1024, 1024)
        pair = (local(k_hbm.at[rows], kv.at[rows]), local(v_hbm.at[rows], vv.at[rows]))
        for cp in pair:
            cp.start()
        kv_loads.append(pair)
    q_load = local(q_hbm, qv)
    q_load.start()
    g_load = local(gate_hbm, gv)
    g_load.start()

    barrier = pltpu.get_barrier_semaphore()
    friends = [sib] + [d[m] for d in (xp, zp, yp) for m in (1, 2, 3)]
    for f in friends:
        pl.semaphore_signal(barrier, inc=1, device_id=f, device_id_type=MESH)

    for c in range(4):
        for cp in kv_loads[c]:
            cp.wait()

        def states(i, carry):
            g = c * 4 + i
            rows = pl.ds(pl.multiple_of(g * GR, GR), GR)
            for h in range(4):
                cols = slice(h * DK, (h + 1) * DK)
                gst[h, g] = lax.dot_general(kv[rows, cols], vv[rows, cols], TN, preferred_element_type=F32)
            return carry

        lax.fori_loop(0, 4, states, 0, unroll=UNROLL)
        for h in range(4):
            p2[h, 2 * c] = gst[h, 4 * c] + gst[h, 4 * c + 1]
            p2[h, 2 * c + 1] = gst[h, 4 * c + 2] + gst[h, 4 * c + 3]
            p4[h, c] = p2[h, 2 * c] + p2[h, 2 * c + 1]
    for h in range(4):
        p8[h, 0] = p4[h, 0] + p4[h, 1]
        p8[h, 1] = p4[h, 2] + p4[h, 3]
        tot[h] = p8[h, 0] + p8[h, 1]

    w_load.wait()
    pl.semaphore_wait(barrier, len(friends))
    mine_h = [2 * core, 2 * core + 1]
    sib_h = [2 * (1 - core), 2 * (1 - core) + 1]
    t_copy = [go([remote(tot.at[h], tsib.at[h], sib)]) for h in sib_h]
    mine = wv.at[z, x, core, pl.ds(pl.multiple_of(y * 16, 16), 16)]
    wy = go([remote(mine, mine, yp[m]) for m in (1, 2, 3)])
    t_copy += [go([remote(tot.at[h], tsib.at[h], sib)]) for h in mine_h]
    c_copy = []
    for i in range(2):
        arrived(t_copy[i])
        cown[i] = tot[mine_h[i]] + tsib[mine_h[i]]
        csend[i] = cown[i].astype(BF16)
        c_copy.append(go([remote(csend.at[i], crecv.at[i, m - 1], xp[m]) for m in (2, 1, 3)]))
    arrived(wy)
    a_own = wv.at[z, x, core, pl.ds(0, 32)]
    b_own = wv.at[z, x, core, pl.ds(32, 32)]
    w1a = go([remote(a_own, a_own, xp[m]) for m in (2, 1, 3)])
    r_copy = []
    for i in range(2):
        arrived(c_copy[i])
        rsend[i] = (
            (cown[i] + crecv[i, 0].astype(F32)) + (crecv[i, 1].astype(F32) + crecv[i, 2].astype(F32))
        ).astype(BF16)
        r_copy.append(go([remote(rsend.at[i], rrecv.at[i, m - 1], zp[m]) for m in (2, 1, 3)]))
    w1b = go([remote(b_own, b_own, zp[m]) for m in (2, 1, 3)])
    x_copy = []
    for i in range(2):
        xfull[0, mine_h[i]] = crecv[i, 0].astype(F32)
        xfull[1, mine_h[i]] = crecv[i, 1].astype(F32) + crecv[i, 2].astype(F32)
        x12 = xfull.at[pl.ds(0, 2), mine_h[i]]
        x_copy += go([remote(x12, x12, sib)])
    for i in range(2):
        arrived(r_copy[i])
        xfull[2, mine_h[i]] = rrecv[i, 0].astype(F32)
        xfull[3, mine_h[i]] = rrecv[i, 1].astype(F32) + rrecv[i, 2].astype(F32)
        x34 = xfull.at[pl.ds(2, 2), mine_h[i]]
        x_copy += go([remote(x34, x34, sib)])
    w2a_src = wv.at[z, :, core, pl.ds(0, 32)]
    w2b_src = wv.at[:, x, core, pl.ds(32, 32)]
    arrived(w1a)
    w2a = go([remote(w2a_src, w2a_src, zp[m]) for m in (2, 1, 3)])
    arrived(x_copy)
    for i in range(2):
        arrived(t_copy[2 + i])
    q_load.wait()

    bits = [core, lax.rem(x, 2), x // 2, lax.rem(z, 2), z // 2]
    cross_bit = [b.astype(F32) for b in bits]
    lane = lax.broadcasted_iota(jnp.int32, (SPAN, DK), 1)
    row = lax.broadcasted_iota(jnp.int32, (SPAN, DK), 0)
    low = lane <= row
    high = lane <= row + SPAN
    left = lane < SPAN

    def attend(g, put):
        rows = pl.ds(pl.multiple_of(g * GR, GR), GR)
        g2, g4, g8 = g // 2, g // 4, g // 8
        own_bit = [lax.rem(b, 2).astype(F32) for b in (g, g2, g4, g8)]
        s1, s2, s4, s8 = flip(g), flip(g2), flip(g4), flip(g8)
        for h in range(4):
            cols = slice(h * DK, (h + 1) * DK)
            qg, kg, vg = qv[rows, cols], kv[rows, cols], vv[rows, cols]
            s = lax.dot_general(qg, kg, NT, preferred_element_type=F32)
            near, far = [], []
            for p in range(GROUP):
                tab = lam[g * GROUP + p]
                w = [lw[l, h, tab] * SCALE[l] for l in range(3)]
                far.append(
                    [lw[3 + i, h, tab] * (SCALE[3 + i] * own_bit[i]) for i in range(4)]
                    + [lw[7 + i, h, tab] * (SCALE[7 + i] * cross_bit[i]) for i in range(5)]
                )
                sp = s[p * SPAN : (p + 1) * SPAN]
                diag = sp[:, (p // 2) * DK : (p // 2 + 1) * DK]
                if p % 2 == 0:
                    diag = jnp.where(low, diag * w[0], 0.0)
                else:
                    diag = jnp.where(high, diag * jnp.where(left, w[1], w[0]), 0.0)
                near.append(
                    diag.astype(BF16)
                    if p < 2
                    else jnp.concatenate([(sp[:, :DK] * w[2]).astype(BF16), diag.astype(BF16)], axis=1)
                )
            part = [
                jnp.dot(jnp.concatenate(near[:2], axis=0), vg[: 2 * SPAN], preferred_element_type=F32),
                jnp.dot(jnp.concatenate(near[2:], axis=0), vg, preferred_element_type=F32),
            ]
            mixed = [[] for _ in range(GROUP)]
            for r in range(0, DK, 32):
                tile = slice(r, r + 32)
                terms = [
                    gst[h, s1, tile, :], p2[h, s2, tile, :], p4[h, s4, tile, :], p8[h, s8, tile, :], tsib[h, tile, :],
                    xfull[0, h, tile, :], xfull[1, h, tile, :], xfull[2, h, tile, :], xfull[3, h, tile, :],
                ]
                for p in range(GROUP):
                    acc = terms[0] * far[p][0]
                    for term, weight in zip(terms[1:], far[p][1:]):
                        acc = acc + term * weight
                    mixed[p].append(acc.astype(BF16))
            res = []
            for p in range(GROUP):
                carried = jnp.dot(
                    qg[p * SPAN : (p + 1) * SPAN], jnp.concatenate(mixed[p], axis=0), preferred_element_type=F32
                )
                res.append((part[p // 2][(p % 2) * SPAN : (p % 2 + 1) * SPAN] + carried).astype(BF16))
            put(cols, rows, jnp.concatenate(res, axis=0))

    def att_copy(j, m):
        g = partner(y, m) * 4 + j
        return pltpu.make_async_remote_copy(
            src_ref=qv.at[pl.ds(pl.multiple_of(g * GR, GR), GR)],
            dst_ref=att.at[y, pl.ds(pl.multiple_of(j * GR, GR), GR)],
            send_sem=att_send.at[j * 3 + m - 1], recv_sem=att_recv.at[j * 3 + m - 1],
            device_id=yp[m], device_id_type=MESH,
        )

    def to_send(cols, rows, value):
        qv[rows, cols] = value

    def attention_round(j):
        def keep(cols, rows, value):
            att[y, pl.ds(pl.multiple_of(j * GR, GR), GR), cols] = value

        for m in (2, 1, 3):
            attend(partner(y, m) * 4 + j, to_send)
            att_copy(j, m).start()
        attend(y * 4 + j, keep)

    def attention_loop(j, carry):
        attention_round(j)
        return carry

    lax.fori_loop(0, 1, attention_loop, 0)
    arrived(w1b)
    w2b = go([remote(w2b_src, w2b_src, xp[m]) for m in (2, 1, 3)])
    fwd = go([remote(c, c, sib) for c in (w2a_src, w2b_src)])
    lax.fori_loop(1, 4, attention_loop, 0)

    for i, m in enumerate((2, 1, 3)):
        arrived([w2a[i], w2b[i]])
        a = wv.at[partner(z, m), :, core, pl.ds(0, 32)]
        b = wv.at[:, partner(x, m), core, pl.ds(32, 32)]
        fwd += go([remote(a, a, sib), remote(b, b, sib)])
    arrived(fwd)
    g_load.wait()

    def normalize(j):
        def tile(i, carry):
            rows = pl.ds(pl.multiple_of(j * GR + i * 16, 16), 16)
            a = jnp.concatenate([att[s, rows, :] for s in range(4)], axis=1).astype(F32)
            gt = gv[rows, :].astype(F32)
            gated = a * (gt / (1.0 + jnp.exp(-gt)))
            mean = jnp.mean(gated * gated, axis=1, keepdims=True)
            nrm[pl.ds(pl.multiple_of(i * 16, 16), 16), :] = (
                gated * lax.rsqrt(mean + 1e-6) * gain[...]
            ).astype(BF16)
            return carry

        lax.fori_loop(0, GR // 16, tile, 0)

    def project_loop(j, carry):
        for m in (1, 2, 3):
            att_copy(j, m).wait_recv()
        normalize(j)
        project(nrm, wv, lambda cols, value: ov.__setitem__((pl.ds(pl.multiple_of(j * GR, GR), GR), cols), value))
        return carry

    lax.fori_loop(0, 3, project_loop, 0)
    for m in (1, 2, 3):
        att_copy(3, m).wait_recv()
    normalize(3)

    for c in everything:
        c.wait_send()
    for j in range(4):
        for m in (1, 2, 3):
            att_copy(j, m).wait_send()


def project(nrm, wv, put):
    for n in range(4):
        value = lax.dot_general(nrm[...], wv[n].reshape(512, 2048), NT, preferred_element_type=F32)
        put(slice(n * 512, (n + 1) * 512), value.astype(BF16))


def last_kernel(ov, nrm, wv, out_hbm, tail, sem):
    stores = [pltpu.make_async_copy(ov.at[pl.ds(j * GR, GR)], out_hbm.at[pl.ds(j * GR, GR)], sem.at[j]) for j in range(3)]
    for c in stores:
        c.start()

    def put(cols, value):
        tail[:, cols] = value

    project(nrm, wv, put)
    stores.append(pltpu.make_async_copy(tail, out_hbm.at[pl.ds(3 * GR, GR)], sem.at[3]))
    stores[3].start()
    for c in stores:
        c.wait()


def local_step(queries, keys, values, lam_index, level_weights, gate, norm_gain, out_weight):
    any_spec = pl.BlockSpec(memory_space=pl.ANY)
    smem = pl.BlockSpec(memory_space=pltpu.SMEM)
    vmem = pl.BlockSpec(memory_space=pltpu.VMEM)
    ov, nrm, wv = pl.pallas_call(
        kernel,
        out_shape=[
            pltpu.VMEM((3 * GR, 2048), BF16),
            pltpu.VMEM((GR, 2048), BF16),
            pltpu.VMEM((4, 4, 2, 64, 2048), BF16),
        ],
        in_specs=[smem, smem, any_spec, any_spec, any_spec, any_spec, vmem, any_spec],
        out_specs=[vmem] * 3,
        scratch_shapes=[
            pltpu.VMEM((4096, 512), BF16),
            pltpu.VMEM((4096, 512), BF16),
            pltpu.VMEM((4096, 512), BF16),
            pltpu.VMEM((1024, 2048), BF16),
            pltpu.VMEM((4, 1024, 512), BF16),
            pltpu.VMEM((4, 16, DK, DK), F32),
            pltpu.VMEM((4, 8, DK, DK), F32),
            pltpu.VMEM((4, 4, DK, DK), F32),
            pltpu.VMEM((4, 2, DK, DK), F32),
            pltpu.VMEM((4, DK, DK), F32),
            pltpu.VMEM((4, DK, DK), F32),
            pltpu.VMEM((2, DK, DK), F32),
            pltpu.VMEM((2, DK, DK), BF16),
            pltpu.VMEM((2, 3, DK, DK), BF16),
            pltpu.VMEM((2, DK, DK), BF16),
            pltpu.VMEM((2, 3, DK, DK), BF16),
            pltpu.VMEM((4, 4, DK, DK), F32),
            pltpu.SemaphoreType.DMA((16,)),
            pltpu.SemaphoreType.DMA((64,)),
            pltpu.SemaphoreType.DMA((64,)),
            pltpu.SemaphoreType.DMA((12,)),
            pltpu.SemaphoreType.DMA((12,)),
        ],
        compiler_params=pltpu.CompilerParams(
            collective_id=0, has_side_effects=True, vmem_limit_bytes=46 * 1024 * 1024
        ),
    )(
        lam_index, jnp.transpose(level_weights, (2, 1, 0)), queries, keys, values, gate,
        norm_gain.reshape(1, 2048), jnp.transpose(out_weight),
    )
    return pl.pallas_call(
        last_kernel,
        out_shape=jax.ShapeDtypeStruct((1024, 2048), BF16),
        in_specs=[vmem] * 3,
        out_specs=any_spec,
        scratch_shapes=[pltpu.VMEM((GR, 2048), BF16), pltpu.SemaphoreType.DMA((4,))],
        compiler_params=pltpu.CompilerParams(vmem_limit_bytes=20 * 1024 * 1024),
    )(ov, nrm, wv)


def solution(mesh):
    in_specs = (
        P("ctx", "head"),
        P("ctx", "head"),
        P("ctx", "head"),
        P("ctx"),
        P(None, "head", None),
        P(("ctx", "head"), None),
        P(),
        P(None, ("ctx", "head")),
    )
    out_specs = P(("ctx", "head"), None)
    return jax.shard_map(local_step, mesh=mesh, in_specs=in_specs, out_specs=out_specs, check_vma=False)
```

```python
import functools

import jax
import jax.numpy as jnp
from jax import lax
from jax.experimental import pallas as pl
from jax.experimental.pallas import tpu as pltpu
from jax.sharding import PartitionSpec as P

DK = 128
SPAN = 64
LEVELS = 12
GROUP = 4
GR = GROUP * SPAN
SCALE = [2.0 ** (-0.5 * l) * DK**-0.5 for l in range(LEVELS)]
MESH = pl.DeviceIdType.MESH
LAST = 3
TAIL = GR
F32 = jnp.float32
UNROLL = True
BF16 = jnp.bfloat16
NT = (((1,), (1,)), ((), ()))
TN = (((0,), (0,)), ((), ()))


def partner(i, m):
    if m == 1:
        return i + 1 - 2 * lax.rem(i, 2)
    if m == 2:
        return i + 2 - 4 * (i // 2)
    return 3 - i


def flip(i):
    return i + 1 - 2 * lax.rem(i, 2)


def kernel(
    lam, lw, q_hbm, k_hbm, v_hbm, gate_hbm, gain, w_hbm, ov, nrm, wv,
    qv, kv, vv, gv, att, gst, p2, p4, p8, tot, tsib, cown, csend, crecv, rsend, rrecv, xfull,
    local_sem, ssem, rsem, att_send, att_recv,
):
    ctx = lax.axis_index("ctx")
    y = lax.axis_index("head")
    core = lax.rem(ctx, 2)
    x = lax.rem(ctx // 2, 4)
    z = ctx // 8

    def dev(zz, xx, cc, yy):
        return (zz * 8 + xx * 2 + cc, yy)

    sib = dev(z, x, 1 - core, y)
    xp = {m: dev(z, partner(x, m), core, y) for m in (1, 2, 3)}
    zp = {m: dev(partner(z, m), x, core, y) for m in (1, 2, 3)}
    yp = {m: dev(z, x, core, partner(y, m)) for m in (1, 2, 3)}

    counter = [0]

    def remote(src, dst, device):
        i = counter[0]
        counter[0] += 1
        return pltpu.make_async_remote_copy(
            src_ref=src, dst_ref=dst, send_sem=ssem.at[i], recv_sem=rsem.at[i],
            device_id=device, device_id_type=MESH,
        )

    lcount = [0]

    def local(src, dst):
        i = lcount[0]
        lcount[0] += 1
        return pltpu.make_async_copy(src, dst, local_sem.at[i])

    everything = []

    def go(copies):
        for c in copies:
            c.start()
        everything.extend(copies)
        return copies

    def arrived(copies):
        for c in copies:
            c.wait_recv()

    w_load = local(w_hbm, wv.at[z, x, core, pl.ds(pl.multiple_of(y * 16, 16), 16)])
    w_load.start()
    kv_loads = []
    for c in range(4):
        rows = pl.ds(c * 1024, 1024)
        pair = (local(k_hbm.at[rows], kv.at[rows]), local(v_hbm.at[rows], vv.at[rows]))
        kv_loads.append(pair)
    for pair in kv_loads[:2]:
        for cp in pair:
            cp.start()
    q_load = local(q_hbm, qv)
    g_load = local(gate_hbm, gv)

    barrier = pltpu.get_barrier_semaphore()
    friends = [sib] + [d[m] for d in (xp, zp, yp) for m in (1, 2, 3)]
    for f in friends:
        pl.semaphore_signal(barrier, inc=1, device_id=f, device_id_type=MESH)

    for c in range(4):
        for cp in kv_loads[c]:
            cp.wait()
        for cp in kv_loads[c + 2] if c < 2 else [q_load] if c == 3 else []:
            cp.start()

        def states(i, carry):
            g = c * 4 + i
            rows = pl.ds(pl.multiple_of(g * GR, GR), GR)
            for h in range(4):
                cols = slice(h * DK, (h + 1) * DK)
                gst[h, g] = lax.dot_general(kv[rows, cols], vv[rows, cols], TN, preferred_element_type=F32)
            return carry

        lax.fori_loop(0, 4, states, 0, unroll=UNROLL)
        for h in range(4):
            p2[h, 2 * c] = gst[h, 4 * c] + gst[h, 4 * c + 1]
            p2[h, 2 * c + 1] = gst[h, 4 * c + 2] + gst[h, 4 * c + 3]
            p4[h, c] = p2[h, 2 * c] + p2[h, 2 * c + 1]
    for h in range(4):
        p8[h, 0] = p4[h, 0] + p4[h, 1]
        p8[h, 1] = p4[h, 2] + p4[h, 3]
        tot[h] = p8[h, 0] + p8[h, 1]

    w_load.wait()
    pl.semaphore_wait(barrier, len(friends))
    mine_h = [core, 2 + core]
    sib_h = [1 - core, 3 - core]
    t_copy = [go([remote(tot.at[h], tsib.at[h], sib)]) for h in sib_h]
    g_load.start()
    mine = wv.at[z, x, core, pl.ds(pl.multiple_of(y * 16, 16), 16)]
    wy = go([remote(mine, mine, yp[m]) for m in (1, 2, 3)])
    t_copy += [go([remote(tot.at[h], tsib.at[h], sib)]) for h in mine_h]
    c_copy = []
    for i in range(2):
        arrived(t_copy[i])
        cown[i] = tot[mine_h[i]] + tsib[mine_h[i]]
        csend[i] = cown[i].astype(BF16)
        c_copy.append(go([remote(csend.at[i], crecv.at[i, m - 1], xp[m]) for m in (2, 1, 3)]))
    arrived(wy)
    a_own = wv.at[z, x, core, pl.ds(0, 32)]
    b_own = wv.at[z, x, core, pl.ds(32, 32)]
    w1a = go([remote(a_own, a_own, xp[m]) for m in (2, 1, 3)])
    r_copy = []
    for i in range(2):
        arrived(c_copy[i])
        rsend[i] = (
            (cown[i] + crecv[i, 0].astype(F32)) + (crecv[i, 1].astype(F32) + crecv[i, 2].astype(F32))
        ).astype(BF16)
        r_copy.append(go([remote(rsend.at[i], rrecv.at[i, m - 1], zp[m]) for m in (2, 1, 3)]))
    w1b = go([remote(b_own, b_own, zp[m]) for m in (2, 1, 3)])
    x_copy = []
    for i in range(2):
        xfull[0, mine_h[i]] = crecv[i, 0].astype(F32)
        xfull[1, mine_h[i]] = crecv[i, 1].astype(F32) + crecv[i, 2].astype(F32)
        x12 = xfull.at[pl.ds(0, 2), mine_h[i]]
        x_copy.append(go([remote(x12, x12, sib)]))
    w2a_src = wv.at[z, :, core, pl.ds(0, 32)]
    w2b_src = wv.at[:, x, core, pl.ds(32, 32)]
    for i in range(2):
        arrived(r_copy[i])
        xfull[2, mine_h[i]] = rrecv[i, 0].astype(F32)
        xfull[3, mine_h[i]] = rrecv[i, 1].astype(F32) + rrecv[i, 2].astype(F32)
        x34 = xfull.at[pl.ds(2, 2), mine_h[i]]
        x_copy[i] += go([remote(x34, x34, sib)])
    arrived(w1a)
    w2a = go([remote(w2a_src, w2a_src, zp[m]) for m in (2, 1, 3)])
    q_load.wait()

    bits = [core, lax.rem(x, 2), x // 2, lax.rem(z, 2), z // 2]
    cross_bit = [b.astype(F32) for b in bits]
    lane = lax.broadcasted_iota(jnp.int32, (SPAN, DK), 1)
    row = lax.broadcasted_iota(jnp.int32, (SPAN, DK), 0)
    low = lane <= row
    high = lane <= row + SPAN
    left = lane < SPAN

    def attend(g, pair, put):
        rows = pl.ds(pl.multiple_of(g * GR, GR), GR)
        g2, g4, g8 = g // 2, g // 4, g // 8
        own_bit = [lax.rem(b, 2).astype(F32) for b in (g, g2, g4, g8)]
        s1, s2, s4, s8 = flip(g), flip(g2), flip(g4), flip(g8)
        for h in (2 * pair, 2 * pair + 1):
            cols = slice(h * DK, (h + 1) * DK)
            qg, kg, vg = qv[rows, cols], kv[rows, cols], vv[rows, cols]
            s = lax.dot_general(qg, kg, NT, preferred_element_type=F32)
            near, far = [], []
            for p in range(GROUP):
                tab = lam[g * GROUP + p]
                w = [lw[l, h, tab] * SCALE[l] for l in range(3)]
                far.append(
                    [lw[3 + i, h, tab] * (SCALE[3 + i] * own_bit[i]) for i in range(4)]
                    + [lw[7 + i, h, tab] * (SCALE[7 + i] * cross_bit[i]) for i in range(5)]
                )
                sp = s[p * SPAN : (p + 1) * SPAN]
                diag = sp[:, (p // 2) * DK : (p // 2 + 1) * DK]
                if p % 2 == 0:
                    diag = jnp.where(low, diag * w[0], 0.0)
                else:
                    diag = jnp.where(high, diag * jnp.where(left, w[1], w[0]), 0.0)
                near.append(
                    diag.astype(BF16)
                    if p < 2
                    else jnp.concatenate([(sp[:, :DK] * w[2]).astype(BF16), diag.astype(BF16)], axis=1)
                )
            part = [
                jnp.dot(jnp.concatenate(near[:2], axis=0), vg[: 2 * SPAN], preferred_element_type=F32),
                jnp.dot(jnp.concatenate(near[2:], axis=0), vg, preferred_element_type=F32),
            ]
            mixed = [[] for _ in range(GROUP)]
            for r in range(0, DK, 32):
                tile = slice(r, r + 32)
                terms = [
                    gst[h, s1, tile, :], p2[h, s2, tile, :], p4[h, s4, tile, :], p8[h, s8, tile, :], tsib[h, tile, :],
                    xfull[0, h, tile, :], xfull[1, h, tile, :], xfull[2, h, tile, :], xfull[3, h, tile, :],
                ]
                for p in range(GROUP):
                    acc = terms[0] * far[p][0]
                    for term, weight in zip(terms[1:], far[p][1:]):
                        acc = acc + term * weight
                    mixed[p].append(acc.astype(BF16))
            res = []
            for p in range(GROUP):
                carried = jnp.dot(
                    qg[p * SPAN : (p + 1) * SPAN], jnp.concatenate(mixed[p], axis=0), preferred_element_type=F32
                )
                res.append((part[p // 2][(p % 2) * SPAN : (p % 2 + 1) * SPAN] + carried).astype(BF16))
            put(cols, rows, jnp.concatenate(res, axis=0))

    def att_copy(j, m, part):
        g = partner(y, m) * 4 + j
        if j is LAST:
            cols, rows, skip = pl.ds(0, 512), GR // 2, part * (GR // 2)
        else:
            cols, rows, skip = pl.ds(part * 256, 256), GR, 0
        return pltpu.make_async_remote_copy(
            src_ref=qv.at[pl.ds(pl.multiple_of(g * GR + skip, 128), rows), cols],
            dst_ref=att.at[y, pl.ds(pl.multiple_of(j * GR + skip, 128), rows), cols],
            send_sem=att_send.at[j * 6 + part * 3 + m - 1], recv_sem=att_recv.at[j * 6 + part * 3 + m - 1],
            device_id=yp[m], device_id_type=MESH,
        )

    def to_send(cols, rows, value):
        qv[rows, cols] = value

    def attention_round(j, ready=None):
        def keep(cols, rows, value):
            att[y, pl.ds(pl.multiple_of(j * GR, GR), GR), cols] = value

        for part in range(2):
            if ready is not None:
                ready(part)
            for m in (2, 1, 3):
                attend(partner(y, m) * 4 + j, part, to_send)
                if j is not LAST:
                    att_copy(j, m, part).start()
        if j is LAST:
            for part in range(2):
                for m in (2, 1, 3):
                    att_copy(j, m, part).start()
        for part in range(2):
            attend(y * 4 + j, part, keep)

    def attention_loop(j, carry):
        attention_round(j)
        return carry

    def ready(part):
        arrived(x_copy[part])
        arrived(t_copy[2 + part])

    attention_round(0, ready)
    arrived(w1b)
    w2b = go([remote(w2b_src, w2b_src, xp[m]) for m in (2, 1, 3)])
    fwd = go([remote(c, c, sib) for c in (w2a_src, w2b_src)])
    lax.fori_loop(1, 3, attention_loop, 0)
    attention_round(LAST)

    def normalize(first, count):
        def tile(i, carry):
            rows = pl.ds(pl.multiple_of(first + i * 16, 16), 16)
            a = jnp.concatenate([att[s, rows, :] for s in range(4)], axis=1).astype(F32)
            gt = gv[rows, :].astype(F32)
            gated = a * (gt * (0.5 + 0.5 * jnp.tanh(0.5 * gt)))
            mean = jnp.mean(gated * gated, axis=1, keepdims=True)
            nrm[rows, :] = (gated * lax.rsqrt(mean + 1e-6) * gain[...]).astype(BF16)
            return carry

        lax.fori_loop(0, count // 16, tile, 0, unroll=2)

    def chunk(first, count):
        rows = pl.ds(pl.multiple_of(first, count), count)

        def put(cols, value):
            ov[rows, cols] = value

        project(nrm.at[rows], wv, put)

    def regrouped(j, parts=(0, 1)):
        for part in parts:
            for m in (1, 2, 3):
                att_copy(j, m, part).wait_recv()

    def project_loop(j, carry):
        chunk(j * GR, GR)
        return carry

    g_load.wait()
    regrouped(0)
    normalize(0, GR)
    for i, m in enumerate((2, 1, 3)):
        arrived([w2a[i], w2b[i]])
        a = wv.at[partner(z, m), :, core, pl.ds(0, 32)]
        b = wv.at[:, partner(x, m), core, pl.ds(32, 32)]
        fwd += go([remote(a, a, sib), remote(b, b, sib)])
    regrouped(1)
    normalize(GR, GR)
    arrived(fwd)
    lax.fori_loop(0, 2, project_loop, 0)
    regrouped(2)
    normalize(2 * GR, GR)
    lax.fori_loop(2, 3, project_loop, 0)
    regrouped(LAST, (0,))
    normalize(3 * GR, GR // 2)
    regrouped(LAST, (1,))
    normalize(3 * GR + GR // 2, GR // 2)

    for c in everything:
        c.wait_send()
    for j in range(4):
        for part in range(2):
            for m in (1, 2, 3):
                att_copy(LAST if j == 3 else j, m, part).wait_send()


def project(nrm, wv, put):
    for n in range(4):
        value = lax.dot_general(nrm[...], wv[n].reshape(512, 2048), NT, preferred_element_type=F32)
        put(slice(n * 512, (n + 1) * 512), value.astype(BF16))


def last_kernel(ov, nrm, wv, out_hbm, tail, sem):
    done = pltpu.make_async_copy(ov, out_hbm.at[pl.ds(0, 1024 - TAIL)], sem.at[0])
    done.start()
    stores = []
    for n in range(4):
        cols = slice(n * 512, (n + 1) * 512)
        value = lax.dot_general(nrm[1024 - TAIL :], wv[n].reshape(512, 2048), NT, preferred_element_type=F32)
        tail[:, cols] = value.astype(BF16)
        stores.append(pltpu.make_async_copy(tail.at[:, cols], out_hbm.at[pl.ds(1024 - TAIL, TAIL), cols], sem.at[1 + n]))
        stores[-1].start()
    for c in [done] + stores:
        c.wait()


def local_step(queries, keys, values, lam_index, level_weights, gate, norm_gain, out_weight):
    any_spec = pl.BlockSpec(memory_space=pl.ANY)
    smem = pl.BlockSpec(memory_space=pltpu.SMEM)
    vmem = pl.BlockSpec(memory_space=pltpu.VMEM)
    ov, nrm, wv = pl.pallas_call(
        kernel,
        out_shape=[
            pltpu.VMEM((1024 - TAIL, 2048), BF16),
            pltpu.VMEM((1024, 2048), BF16),
            pltpu.VMEM((4, 4, 2, 64, 2048), BF16),
        ],
        in_specs=[smem, smem, any_spec, any_spec, any_spec, any_spec, vmem, any_spec],
        out_specs=[vmem] * 3,
        scratch_shapes=[
            pltpu.VMEM((4096, 512), BF16),
            pltpu.VMEM((4096, 512), BF16),
            pltpu.VMEM((4096, 512), BF16),
            pltpu.VMEM((1024, 2048), BF16),
            pltpu.VMEM((4, 1024, 512), BF16),
            pltpu.VMEM((4, 16, DK, DK), F32),
            pltpu.VMEM((4, 8, DK, DK), F32),
            pltpu.VMEM((4, 4, DK, DK), F32),
            pltpu.VMEM((4, 2, DK, DK), F32),
            pltpu.VMEM((4, DK, DK), F32),
            pltpu.VMEM((4, DK, DK), F32),
            pltpu.VMEM((2, DK, DK), F32),
            pltpu.VMEM((2, DK, DK), BF16),
            pltpu.VMEM((2, 3, DK, DK), BF16),
            pltpu.VMEM((2, DK, DK), BF16),
            pltpu.VMEM((2, 3, DK, DK), BF16),
            pltpu.VMEM((4, 4, DK, DK), F32),
            pltpu.SemaphoreType.DMA((16,)),
            pltpu.SemaphoreType.DMA((64,)),
            pltpu.SemaphoreType.DMA((64,)),
            pltpu.SemaphoreType.DMA((24,)),
            pltpu.SemaphoreType.DMA((24,)),
        ],
        compiler_params=pltpu.CompilerParams(
            collective_id=0, has_side_effects=True, vmem_limit_bytes=46 * 1024 * 1024
        ),
    )(
        lam_index, jnp.transpose(level_weights, (2, 1, 0)), queries, keys, values, gate,
        norm_gain.reshape(1, 2048), jnp.transpose(out_weight),
    )
    return pl.pallas_call(
        last_kernel,
        out_shape=jax.ShapeDtypeStruct((1024, 2048), BF16),
        in_specs=[vmem] * 3,
        out_specs=any_spec,
        scratch_shapes=[pltpu.VMEM((TAIL, 2048), BF16), pltpu.SemaphoreType.DMA((5,))],
        compiler_params=pltpu.CompilerParams(vmem_limit_bytes=20 * 1024 * 1024),
    )(ov, nrm, wv)


def solution(mesh):
    in_specs = (
        P("ctx", "head"),
        P("ctx", "head"),
        P("ctx", "head"),
        P("ctx"),
        P(None, "head", None),
        P(("ctx", "head"), None),
        P(),
        P(None, ("ctx", "head")),
    )
    out_specs = P(("ctx", "head"), None)
    return jax.shard_map(local_step, mesh=mesh, in_specs=in_specs, out_specs=out_specs, check_vma=False)
```
